128 devices in a mesh: seq: 16 (over x, z_hi, core), res: 8 (over y, z_lo).
Axes of the slice: x: 4, y: 4, z: 4 (z_hi: 2, z_lo: 2; z = z_hi * 2 + z_lo), core: 2. Of those that a mesh axis runs over, the one named last changes fastest.
Arguments:
- homolog_embedding: bfloat16 [512, 768, 256], P('seq', 'res'), may hold values from -6 to 6
- homolog_entry_flags: int32 [512, 768], P('seq', 'res'), may hold values 0 or 1
- amino_exists_flags: int32 [768], P('res'), may hold values 0 or 1
- couple_embedding: bfloat16 [768, 768, 128], P('res', 'seq'), may hold values from -6 to 6
- couple_layernorm_scale: float32 [128], replicated, may hold values from 0.1 to 1.9
- couple_offset_matrix: bfloat16 [128, 8], replicated, may hold values from -0.5 to 0.5
- horizontal_layernorm_scale: float32 [256], replicated, may hold values from 0.1 to 1.9
- horizontal_qkvg_matrix: bfloat16 [4, 256, 256], replicated, may hold values from -9 to 9
- horizontal_final_matrix: bfloat16 [256, 256], replicated, may hold values from -4 to 4
- vertical_layernorm_scale: float32 [256], replicated, may hold values from 0.1 to 1.9
- vertical_qkvg_matrix: bfloat16 [4, 256, 256], replicated, may hold values from -9 to 9
- vertical_final_matrix: bfloat16 [256, 256], replicated, may hold values from -4 to 4
Outputs:
- horizontal_increment: bfloat16 [512, 768, 256], P('seq', 'res')
- col_update: bfloat16 [512, 768, 256], P('seq', 'res')
The draws below stay inside these ranges and needn't reach their ends.
All inputs are finite; a program needn't handle non-finite values. No bound on the sum of `homolog_entry_flags` or of `amino_exists_flags` on one device may be relied on, other than what follows from the above.
Results may differ from the reference program's by a relative error of at most 0.02.
The reference program's roundings to bfloat16 on the way count: a program that leaves them out, or rounds other values in their place, can miss the bound.
Values may be sent and summed in bfloat16 or wider, within the bound.
A program may use at most 128 MiB of HBM per device.

```python
import jax
import jax.numpy as jnp
from jax import lax

FEATURE_DEPTH = 256
CZ = 128
HEAD_TOTAL = 8
PER_HEAD_DEPTH = 32
HOMOLOG_TOTAL = 512
CHAIN_LENGTH = 768


def tied_projection(key):
    leading_factor = jax.random.fold_in(key, 0)
    starting_tensor = jax.random.normal(leading_factor, (4, FEATURE_DEPTH, FEATURE_DEPTH), jnp.float32)
    asking_vectors = starting_tensor[0]
    complete_tensor = jnp.concatenate([asking_vectors[None], starting_tensor[1:]], axis=0) * FEATURE_DEPTH ** (-0.5)
    return jnp.clip(complete_tensor, -9.0, 9.0).astype(jnp.bfloat16)


def draw_horizontal_qkvg_matrix(key, part):
    key = jax.random.fold_in(key, 5)
    return tied_projection(key)


def draw_vertical_qkvg_matrix(key, part):
    key = jax.random.fold_in(key, 9)
    return tied_projection(key)


def set_ends(values, key, smallest, high):
    longest = values.shape.index(max(values.shape))
    spots = []
    for shift in (0, 1):
        where = [jax.random.randint(jax.random.fold_in(key, axis), (), 0, length) for axis, length in enumerate(values.shape)]
        where[longest] = (where[longest] + shift) % values.shape[longest]
        spots.append(tuple(where))
    return values.at[spots[0]].set(smallest).at[spots[1]].set(high)


def steps_of(rng, dims, pieces, smallest, top_value):
    level = 1.0
    for dim, blocks in pieces:
        draws = jax.random.uniform(jax.random.fold_in(jax.random.fold_in(rng, 6), dim), (blocks,), jnp.float32, smallest / len(pieces), top_value / len(pieces))
        level = level * jnp.repeat(jnp.exp(draws), dims[dim] // blocks).reshape((-1,) + (1,) * (len(dims) - 1 - dim))
    return level


def bell_draw(stream_key, extent, deviation, reach, shards=(), dtype=jnp.bfloat16):
    loudness = steps_of(stream_key, extent, shards, -0.22, 0.18) if shards else 1.0
    result = jax.random.normal(stream_key, extent, jnp.float32) * deviation * loudness
    return jnp.minimum(jnp.maximum(result, -reach), reach).astype(dtype)


def setup_inputs(seed: int = 0) -> dict:
    streams_of = jax.random.split(jax.random.key(seed), 13)
    homolog_embedding = bell_draw(streams_of[0], (HOMOLOG_TOTAL, CHAIN_LENGTH, FEATURE_DEPTH), 1.0, 6.0, ((0, 16), (1, 8)))
    homolog_entry_flags = set_ends((jax.random.randint(streams_of[1], (HOMOLOG_TOTAL, CHAIN_LENGTH), 0, 8) < 7).astype(jnp.int32), jax.random.fold_in(streams_of[1], 1), 0, 1)
    amino_exists_flags = set_ends((jax.random.randint(streams_of[2], (CHAIN_LENGTH,), 0, 16) < 15).astype(jnp.int32), jax.random.fold_in(streams_of[2], 1), 0, 1)
    couple_embedding = bell_draw(streams_of[3], (CHAIN_LENGTH, CHAIN_LENGTH, CZ), 1.0, 6.0, ((0, 8), (1, 16)))
    couple_layernorm_scale = jnp.clip(1.0 + 0.18 * jax.random.normal(streams_of[4], (CZ,), jnp.float32), 0.1, 1.9)
    couple_offset_matrix = bell_draw(streams_of[5], (CZ, HEAD_TOTAL), CZ ** -0.5, 0.5)
    horizontal_layernorm_scale = jnp.clip(1.0 + 0.18 * jax.random.normal(streams_of[6], (FEATURE_DEPTH,), jnp.float32), 0.1, 1.9)
    horizontal_qkvg_matrix = draw_horizontal_qkvg_matrix(jax.random.fold_in(streams_of[12], 71), 0)
    horizontal_final_matrix = bell_draw(streams_of[8], (FEATURE_DEPTH, FEATURE_DEPTH), 1.0, 4.0)
    vertical_layernorm_scale = jnp.clip(1.0 + 0.18 * jax.random.normal(streams_of[9], (FEATURE_DEPTH,), jnp.float32), 0.1, 1.9)
    vertical_qkvg_matrix = draw_vertical_qkvg_matrix(jax.random.fold_in(streams_of[12], 71), 0)
    vertical_final_matrix = bell_draw(streams_of[11], (FEATURE_DEPTH, FEATURE_DEPTH), 1.0, 4.0)
    return dict(homolog_embedding=homolog_embedding, homolog_entry_flags=homolog_entry_flags, amino_exists_flags=amino_exists_flags, couple_embedding=couple_embedding, couple_layernorm_scale=couple_layernorm_scale, couple_offset_matrix=couple_offset_matrix, horizontal_layernorm_scale=horizontal_layernorm_scale, horizontal_qkvg_matrix=horizontal_qkvg_matrix, horizontal_final_matrix=horizontal_final_matrix, vertical_layernorm_scale=vertical_layernorm_scale, vertical_qkvg_matrix=vertical_qkvg_matrix, vertical_final_matrix=vertical_final_matrix)


def widen(array):
    return lax.optimization_barrier(array).astype(jnp.float32)

def normalize(inputs, gain_vec):
    floats = widen(inputs)
    centre = lax.optimization_barrier(jnp.mean(floats, axis=-1, keepdims=True))
    spread = lax.optimization_barrier(jnp.mean(jnp.square(floats - centre), axis=-1, keepdims=True))
    return ((floats - centre) * lax.rsqrt(spread + 1e-05) * gain_vec).astype(jnp.bfloat16)

def attend(projected, key_present, pair_bias):
    asking_vectors = widen(projected[:, :, 0])
    key_rows = widen(projected[:, :, 1])
    values = widen(projected[:, :, 2])
    gate_logit = widen(projected[:, :, 3])
    scores = jnp.einsum('ihd,jhd->hij', asking_vectors, key_rows) * PER_HEAD_DEPTH ** (-0.5)
    scores = scores + (key_present.astype(jnp.float32) - 1.0)[None, None, :] * 1000000000.0
    if pair_bias is not None:
        scores = scores + pair_bias.astype(jnp.float32)
    peak = lax.optimization_barrier(jnp.max(scores, axis=-1, keepdims=True))
    powers = jnp.exp(scores - peak)
    totals = lax.optimization_barrier(jnp.sum(powers, axis=-1))
    mixture = jnp.einsum('hij,jhd->ihd', widen(powers.astype(jnp.bfloat16)), values)
    mixture = mixture / jnp.transpose(totals)[:, :, None]
    return (jax.nn.sigmoid(gate_logit) * mixture).astype(jnp.bfloat16)

def reference(homolog_embedding, homolog_entry_flags, amino_exists_flags, couple_embedding, couple_layernorm_scale, couple_offset_matrix, horizontal_layernorm_scale, horizontal_qkvg_matrix, horizontal_final_matrix, vertical_layernorm_scale, vertical_qkvg_matrix, vertical_final_matrix):
    pair_norm = normalize(couple_embedding, couple_layernorm_scale)
    bias_full = jnp.einsum('ijc,ch->hij', widen(pair_norm), couple_offset_matrix.astype(jnp.float32)).astype(jnp.bfloat16)
    horizontal_probabilities = horizontal_qkvg_matrix.astype(jnp.float32).reshape(4, FEATURE_DEPTH, HEAD_TOTAL, PER_HEAD_DEPTH)
    horizontal_exists = (homolog_entry_flags * amino_exists_flags[None, :]).astype(jnp.float32)

    def horizontal_lone(element):
        sequence, live_keys = element
        normed = normalize(sequence, horizontal_layernorm_scale)
        projected = jnp.einsum('rc,achd->rhad', widen(normed), horizontal_probabilities).astype(jnp.bfloat16)
        sigmoid_scaled = attend(projected, live_keys, bias_full)
        return jnp.dot(sigmoid_scaled.reshape(CHAIN_LENGTH, FEATURE_DEPTH), horizontal_final_matrix, preferred_element_type=jnp.float32).astype(jnp.bfloat16)
    horizontal_increment = lax.map(horizontal_lone, (homolog_embedding, horizontal_exists))
    vertical_source = (homolog_embedding.astype(jnp.float32) + horizontal_increment.astype(jnp.float32)).astype(jnp.bfloat16)
    vertical_probabilities = vertical_qkvg_matrix.astype(jnp.float32).reshape(4, FEATURE_DEPTH, HEAD_TOTAL, PER_HEAD_DEPTH)

    def column_single(element):
        column, live_keys = element
        normed = normalize(column, vertical_layernorm_scale)
        projected = jnp.einsum('sc,achd->shad', widen(normed), vertical_probabilities).astype(jnp.bfloat16)
        sigmoid_scaled = attend(projected, live_keys, None)
        return jnp.dot(sigmoid_scaled.reshape(HOMOLOG_TOTAL, FEATURE_DEPTH), vertical_final_matrix, preferred_element_type=jnp.float32).astype(jnp.bfloat16)
    column_output = lax.map(column_single, (jnp.transpose(vertical_source, (1, 0, 2)), jnp.transpose(homolog_entry_flags).astype(jnp.float32)))
    col_update = jnp.transpose(column_output, (1, 0, 2))
    return (horizontal_increment, col_update)
```

```python
import jax
import jax.numpy as jnp
from jax import lax
from jax.experimental import pallas as pl
from jax.experimental.pallas import tpu as pltpu
from jax.sharding import PartitionSpec as P

F32 = jnp.float32
BF = jnp.bfloat16
MESH = pl.DeviceIdType.MESH
HEADS = 8
WIDTH = 32
CHAN = 256
QROWS = 64
LOG2E = 1.4426950408889634
VLIM = 63 * 2**20


def nt(a, b):
    return lax.dot_general(a, b, (((1,), (1,)), ((), ())), preferred_element_type=F32)


def tn(a, b):
    return lax.dot_general(a, b, (((0,), (0,)), ((), ())), preferred_element_type=F32)


def nn(a, b):
    return lax.dot_general(a, b, (((1,), (0,)), ((), ())), preferred_element_type=F32)


def norm(x, gain):
    f = x.astype(F32)
    c = f - jnp.mean(f, axis=-1, keepdims=True)
    v = jnp.mean(c * c, axis=-1, keepdims=True)
    return (c * lax.rsqrt(v + 1e-5) * gain).astype(BF)


def peak_of(a):
    n = a.shape[0]
    while n > 8 and n % 16 == 0:
        n //= 2
        a = jnp.maximum(a[:n], a[n:])
    top = a[:8]
    for i in range(8, n, 8):
        top = jnp.maximum(top, a[i:i + 8])
    return jnp.max(top, axis=0, keepdims=True)


def project(x, gain, col, wk_ref, wt_ref, keys, asks, pick_asks, xn_s, k_s, q_s, v_s, g_s):
    xn = norm(x, gain)
    xn_s[...] = xn
    lane = lax.broadcasted_iota(jnp.int32, (x.shape[0], 128), 1)
    add = jnp.where(lane == WIDTH, col, 0.0)
    add = jnp.concatenate([add, add], axis=1)
    for h in range(0, HEADS, 2):
        at = slice(h * 128, (h + 2) * 128)
        key = (nn(xn, wk_ref[:, at]) + add).astype(BF)
        for lo, n, to in keys:
            k_s[pl.ds(to, n), at] = key[lo:lo + n]
    vt = nt(wt_ref[1], xn).astype(BF)
    for lo, n, to in keys:
        for h in range(HEADS):
            v_s[h, :WIDTH, pl.ds(to, n)] = vt[h * WIDTH:(h + 1) * WIDTH, lo:lo + n]
    xq = pick_asks(xn_s)
    qt = (nt(wt_ref[0], xq) * (WIDTH ** -0.5 * LOG2E)).astype(BF)
    gt = nt(wt_ref[2], xq).astype(BF)
    for lo, n, to in asks:
        g_s[:, pl.ds(to, n)] = gt[:, lo:lo + n]
        for h in range(HEADS):
            q_s[h, :WIDTH, pl.ds(to, n)] = qt[h * WIDTH:(h + 1) * WIDTH, lo:lo + n]


def attend(klo, nk, qlo, nq, bias_ref, k_s, q_s, v_s, g_s, o_s):
    keys, cols = pl.ds(klo, nk), pl.ds(qlo, nq)

    def score(h):
        sc = nn(k_s[keys, h * 128:h * 128 + QROWS], q_s[h, :, cols])
        return sc if bias_ref is None else sc + bias_ref[h]

    sc = score(0)
    for h in range(HEADS):
        ahead = score(h + 1) if h + 1 < HEADS else None
        p = jnp.exp2(sc - peak_of(sc)).astype(BF)
        o = nn(v_s[h, :, keys], p)
        at = slice(h * WIDTH, (h + 1) * WIDTH)
        gate = jax.nn.sigmoid(g_s[at, cols].astype(F32))
        o_s[at, cols] = (gate * (o[:WIDTH] * (1.0 / o[WIDTH:WIDTH + 1]))).astype(BF)
        sc = ahead


def pick(table, which):
    at = lax.broadcasted_iota(jnp.int32, table.shape, 1) == which
    return jnp.sum(jnp.where(at, table, 0.0), axis=1, keepdims=True)


def kernel(pair_hbm, pgain_ref, pw_ref, own_hbm, flags_ref, amino_ref, rgain_ref, rw_hbm, ro_ref, cgain_ref, cw_hbm, co_ref,
           inc_hbm, fin_hbm,
           pair_ref, own_ref, rw_ref, cw_ref, inc_ref, perm_s, buf, bias_s, turn_s, rsend_ref, csend_ref, rows_s, rmask_s, cmask_s, col_s, out_s, done_s, ctab_s, xn_s,
           k_s, q_s, v_s, g_s, o_s, wk_s, wt_s,
           gsend, grecv, psend, precv, ysend, yrecv, zsend, zrecv, bsend, brecv, csend, crecv, esend, erecv,
           rmsend, rmrecv, cmsend, cmrecv, lsem, tsem):
    s_me = lax.axis_index("seq")
    r_me = lax.axis_index("res")
    x, zhi, c = s_me // 4, (s_me // 2) % 2, s_me % 2
    y, zlo = r_me // 2, r_me % 2

    def along_x(d):
        return ((x + d) % 4 * 4 + zhi * 2 + c, r_me)

    def along_y(d):
        return (s_me, (y + d) % 4 * 2 + zlo)

    far = (x * 4 + (1 - zhi) * 2 + c, r_me)
    near = (s_me, y * 2 + 1 - zlo)
    twin = (x * 4 + zhi * 2 + 1 - c, r_me)

    def res_peer(k):
        return (s_me, (r_me + k) % 8)

    def seq_peer(k):
        return ((s_me + k) % 16, r_me)

    def remote(src, dst, ssem, rsem, to):
        return pltpu.make_async_remote_copy(src, dst, ssem, rsem, device_id=to, device_id_type=MESH)

    own_rows = pl.ds(pl.multiple_of(r_me * 96, 96), 96)

    def all_sent(ref, sem):
        remote(ref, ref, sem, sem, twin).wait_send()

    def all_here(ref, sem):
        remote(ref, ref, sem, sem, twin).wait_recv()

    loads = [pltpu.make_async_copy(src, dst, lsem.at[i]) for i, (src, dst) in enumerate((
        (pair_hbm, pair_ref), (own_hbm.at[pl.ds(8 * y, 8)], rows_s.at[:, own_rows]), (rw_hbm, rw_ref), (cw_hbm, cw_ref),
        (own_hbm, own_ref)))]
    for load in loads:
        load.start()
    barrier = pltpu.get_barrier_semaphore()
    for k in range(1, 8):
        pl.semaphore_signal(barrier, inc=1, device_id=res_peer(k), device_id_type=MESH)
    for k in range(1, 16):
        pl.semaphore_signal(barrier, inc=1, device_id=seq_peer(k), device_id_type=MESH)
    rsend_ref[...] = jnp.zeros_like(rsend_ref)
    csend_ref[...] = jnp.zeros_like(csend_ref)
    live = ((flags_ref[...] * amino_ref[...]).astype(F32) - 1.0) * (1e9 * LOG2E)
    for b in range(4):
        rsend_ref[b, :, :96] = live[8 * b:8 * b + 8]
    lines = [flags_ref[8 * b + i:8 * b + i + 1, :] for i in range(8) for b in range(4)]
    seen = jnp.concatenate(lines, axis=0)
    seen = jnp.concatenate([(seen.astype(F32) - 1.0) * (1e9 * LOG2E), jnp.zeros((32, 32), F32)], axis=1)
    seen = jnp.transpose(seen)
    for a in range(16):
        csend_ref[a, :6, :32] = seen[6 * a:6 * a + 6]
    pl.semaphore_wait(barrier, 22)

    ALONG = ((along_x, along_y), (along_y, along_x))
    PLACE = ((x, y), (y, x))

    def region(p, phase, last=None):
        a, b = PLACE[p]
        if phase == 0:
            return buf.at[p, a, b, zhi, c]
        if phase == 1:
            return buf.at[p, a, b, :, c]
        return buf.at[p, :, (b if last is None else last), :, c]

    def ring(p, phase, d):
        at = region(p, phase)
        to = far if phase == 0 else ALONG[p][phase - 1](d)
        return remote(at, at, gsend.at[p, phase, d - 1], grecv.at[p, phase, d - 1], to)

    def pair(p, d):
        at = region(p, 2, (PLACE[p][1] - d) % 4)
        return remote(at, at, psend.at[p, d], precv.at[p, d], twin)

    def steps(phase):
        return (1,) if phase == 0 else (1, 3, 2)

    def start_rings(phase):
        for p in range(2):
            for d in steps(phase):
                ring(p, phase, d).start()

    def end_rings(phase):
        for p in range(2):
            for d in steps(phase):
                ring(p, phase, d).wait_recv()

    def y_copy(half, d):
        return remote(own_hbm.at[pl.ds((y + d) % 4 * 8 + 4 * half, 4)], rows_s.at[pl.ds(4 * half, 4), own_rows],
                      ysend.at[half, d], yrecv.at[half, d], along_y(d))

    def z_copy(half, d):
        at = rows_s.at[pl.ds(4 * half, 4), pl.ds(pl.multiple_of(((y - d) % 4 * 2 + zlo) * 96, 96), 96)]
        src = own_hbm.at[pl.ds(y * 8 + 4 * half, 4)] if d == 0 else at
        return remote(src, at, zsend.at[half, d], zrecv.at[half, d], near)

    def row_flags(k):
        return remote(rsend_ref.at[(r_me + k) % 8 // 2], rmask_s.at[r_me], rmsend, rmrecv, res_peer(k))

    def col_flags(k):
        return remote(csend_ref.at[(s_me + k) % 16], cmask_s.at[s_me], cmsend, cmrecv, seq_peer(k))

    z_copy(0, 0).start()
    for d in (1, 3, 2):
        y_copy(0, d).start()
    for k in range(1, 8):
        row_flags(k).start()

    loads[0].wait()
    pw = jnp.transpose(pw_ref[...].astype(F32)).astype(BF)
    flat = nt(pw, norm(pair_ref[...].reshape(4608, 128), pgain_ref[...]))
    for i in range(96):
        turn_s[i * 8:(i + 1) * 8, :48] = flat[:, i * 48:(i + 1) * 48]
    for p in range(2):
        a, b = PLACE[p]
        heads = [jnp.transpose(turn_s[pl.ds(4 * p + h, 96, stride=8), :])[:48] for h in range(4)]
        for m in range(3):
            both = jnp.concatenate([heads[m], heads[3][:, m * 32:(m + 1) * 32]], axis=1)
            buf[p, a, b, zhi, c, m * 48:(m + 1) * 48] = both.astype(BF)
    start_rings(0)

    rmask_s[r_me] = rsend_ref[y]
    cmask_s[s_me] = csend_ref[s_me]
    for load in loads[1:]:
        load.wait()
    for i, (w_ref, at) in enumerate(((rw_ref, 0), (cw_ref, 1))):
        wk_s[at] = jnp.zeros((CHAN, HEADS * 128), BF)
        for h in range(HEADS):
            wk_s[at, :, h * 128:h * 128 + WIDTH] = w_ref[1, :, h * WIDTH:(h + 1) * WIDTH]
        for j, m in enumerate((0, 2, 3)):
            wt_s[at, j] = jnp.transpose(w_ref[m].astype(F32)).astype(BF)
    one = lax.broadcasted_iota(jnp.int32, (QROWS - WIDTH, 3072), 0) == 0
    ones = jnp.where(one, 1.0, 0.0).astype(BF)
    for h in range(HEADS):
        q_s[h, WIDTH:, :] = ones
        v_s[h, WIDTH:, :] = jnp.ones((16, 6144), BF)
    for d in (1, 3, 2):
        y_copy(0, d).wait_recv()
        z_copy(0, d).start()
    for d in (1, 3, 2):
        y_copy(1, d).start()
    end_rings(0)
    start_rings(1)
    z_copy(1, 0).start()
    spot = lax.broadcasted_iota(jnp.int32, (512, 512), 0)
    line = spot % 32
    spot = line % 8 // 2 * 128 + spot // 32 * 8 + line % 2 * 4 + line // 8
    perm_s[...] = jnp.where(lax.broadcasted_iota(jnp.int32, (512, 512), 1) == spot, 1.0, 0.0).astype(BF)
    end_rings(1)
    start_rings(2)
    for p in range(2):
        pair(p, 0).start()
    for k in range(1, 16):
        col_flags(k).start()
    all_here(rmask_s.at[pl.ds(0, 7)], rmrecv)
    for d in range(4):
        z_copy(0, d).wait_recv()
    rtab = jnp.transpose(jnp.concatenate([rmask_s[b][:, :96] for b in range(8)], axis=1))

    def own_queries(ref):
        return jnp.concatenate([ref[pl.ds(pl.multiple_of((2 * b + zlo) * 96, 96), 96)] for b in range(4)], axis=0)

    def row_project(s, _):
        project(rows_s[s], rgain_ref[...], pick(rtab, s), wk_s.at[0], wt_s.at[0],
                [(0, 768, pl.multiple_of(s * 768, 256))], [(0, 384, pl.multiple_of(s * 384, 128))], own_queries,
                xn_s, k_s, q_s, v_s, g_s)
        return 0

    lax.fori_loop(0, 4, row_project, 0)

    for d in (1, 3, 2):
        for p in range(2):
            ring(p, 2, d).wait_recv()
            pair(p, d).start()
    for p in range(2):
        for d in range(4):
            pair(p, d).wait_recv()

    def scaled(b):
        return b.astype(F32) * LOG2E

    def assemble(s, _):
        at = pl.ds(pl.multiple_of(s * 48, 16), 48)
        for p in range(2):
            got = []
            for b in range(4):
                one, two = (s // 4, b) if p == 0 else (b, s // 4)
                got.append(buf[p, one, two, (s // 2) % 2, s % 2])
            for m in range(3):
                bias_s[4 * p + m, at, :] = scaled(jnp.concatenate([g[m * 48:(m + 1) * 48, :96] for g in got], axis=1))
            bias_s[4 * p + 3, at, :] = scaled(jnp.concatenate(
                [g[m * 48:(m + 1) * 48, 96:] for g in got for m in range(3)], axis=1))
        return 0

    lax.fori_loop(0, 16, assemble, 0)

    def back_copy(s, d):
        at = pl.ds(pl.multiple_of(s * 384 + (y + d) % 4 * 96, 96), 96)
        return remote(done_s.at[at], inc_ref.at[8 * y + s], bsend.at[s], brecv.at[s], along_y(d))

    def col_copy(s, k):
        return remote(out_s.at[s, (s_me + k) % 16], col_s.at[s_me, s], csend.at[s], crecv.at[s], seq_peer(k))

    def owner(s):
        for u in range(2):
            all_here(done_s.at[pl.ds(0, 288)], brecv.at[2 * s + u])
        parts = []
        for p in range(8):
            line = p % 4 * 8 + 2 * s + p // 4
            parts.append(own_ref[line].astype(F32) + inc_ref[line].astype(F32))
        both = jnp.swapaxes(jnp.stack(parts), 0, 1)
        out_s[s] = both.reshape(16, 48, CHAN).astype(BF)
        for k in range(1, 16):
            col_copy(s, k).start()
        col_s[s_me, s] = out_s[s, s_me]

    def row_step(s, _):
        lo = pl.multiple_of(s * 384, 128)
        attend(pl.multiple_of(s * 768, 256), 768, lo, 384, bias_s, k_s, q_s, v_s, g_s, o_s)
        done_s[pl.ds(lo, 384)] = tn(o_s[:, pl.ds(lo, 384)], ro_ref[...]).astype(BF)
        for d in (1, 3, 2):
            back_copy(s, d).start()
        inc_ref[8 * y + s] = done_s[pl.ds(pl.multiple_of(s * 384 + y * 96, 96), 96)]

        @pl.when(s == 0)
        def _():
            for d in (1, 3, 2):
                y_copy(1, d).wait_recv()
                z_copy(1, d).start()

        @pl.when(s == 3)
        def _():
            for d in range(4):
                z_copy(1, d).wait_recv()
            lax.fori_loop(4, 8, row_project, 0)

        @pl.when((s % 2 == 0) & (s > 0))
        def _():
            owner(s // 2 - 1)
        return 0

    lax.fori_loop(0, 8, row_step, 0)

    keep = pltpu.make_async_copy(inc_ref, inc_hbm, lsem.at[0])
    all_here(cmask_s.at[pl.ds(0, 15)], cmrecv)
    for a in range(16):
        turned = jnp.transpose(cmask_s[a])
        for s in range(4):
            ctab_s[s, a * 8:(a + 1) * 8, :8] = turned[s * 8:(s + 1) * 8]

    def col_project(s, _):
        all_here(out_s.at[s, pl.ds(0, 15)], crecv.at[s])
        six = col_s[:, s].astype(F32).reshape(16, 6, 8, CHAN)
        six = jnp.concatenate([six[:, r].reshape(128, CHAN) for r in range(6)], axis=0)
        tab = ctab_s[s]
        flag = jnp.concatenate([tab[:, r:r + 1] for r in range(6)], axis=0)
        spots = [(r * 128, 128, pl.multiple_of(r * 512 + s * 128, 128)) for r in range(6)]
        project(six, cgain_ref[...], flag, wk_s.at[1], wt_s.at[1],
                spots, spots, lambda ref: ref[...], xn_s, k_s, q_s, v_s, g_s)
        return 0

    lax.fori_loop(0, 2, col_project, 0)
    owner(3)
    keep.start()
    lax.fori_loop(2, 4, col_project, 0)

    def free(s, _):
        all_sent(done_s.at[pl.ds(0, 288)], bsend.at[s])
        return 0

    lax.fori_loop(0, 8, free, 0)

    def end_copy(r, k):
        to = (s_me + k) % 16
        at = pl.ds(pl.multiple_of(r * 512 + to * 32, 32), 32)
        return remote(done_s.at[at], fin_hbm.at[s_me, r], esend.at[r], erecv.at[r], seq_peer(k))

    def own_end(r):
        at = pl.ds(pl.multiple_of(r * 512 + s_me * 32, 32), 32)
        return pltpu.make_async_copy(done_s.at[at], fin_hbm.at[s_me, r], tsem.at[r])

    def col_step(r, _):
        lo = pl.multiple_of(r * 512, 512)
        attend(lo, 512, lo, 512, None, k_s, q_s, v_s, g_s, o_s)
        y = tn(o_s[:, pl.ds(lo, 512)], co_ref[...])
        done_s[pl.ds(lo, 512)] = nn(perm_s[...], y.astype(BF)).astype(BF)
        for k in range(1, 16):
            end_copy(r, k).start()
        own_end(r).start()
        return 0

    lax.fori_loop(0, 6, col_step, 0)

    all_sent(rmask_s.at[pl.ds(0, 7)], rmsend)
    all_sent(cmask_s.at[pl.ds(0, 15)], cmsend)
    for half in range(2):
        for d in range(1, 4):
            y_copy(half, d).wait_send()
        for d in range(4):
            z_copy(half, d).wait_send()
    for p in range(2):
        for phase in range(3):
            for d in steps(phase):
                ring(p, phase, d).wait_send()
        for d in range(4):
            pair(p, d).wait_send()

    def drain_cols(s, _):
        all_sent(out_s.at[s, pl.ds(0, 15)], csend.at[s])
        return 0

    lax.fori_loop(0, 4, drain_cols, 0)

    def drain(r, _):
        all_sent(done_s.at[pl.ds(0, 480)], esend.at[r])
        all_here(done_s.at[pl.ds(0, 480)], erecv.at[r])
        own_end(r).wait()
        return 0

    lax.fori_loop(0, 6, drain, 0)
    keep.wait()


def call(pair, pgain, pw, own, flags, amino, rgain, rw, ro, cgain, cw, co):
    args = (pair, pgain, pw, own, flags, amino, rgain, rw, ro, cgain, cw, co)
    dma = pltpu.SemaphoreType.DMA
    vmem = pl.BlockSpec(memory_space=pltpu.VMEM)
    hbm = pl.BlockSpec(memory_space=pl.ANY)
    return pl.pallas_call(
        kernel,
        out_shape=(jax.ShapeDtypeStruct((32, 96, CHAN), BF), jax.ShapeDtypeStruct((16, 6, 32, CHAN), BF)),
        in_specs=[hbm if i in (0, 3, 7, 10) else vmem for i in range(len(args))],
        out_specs=(hbm, hbm),
        scratch_shapes=[
            pltpu.VMEM((96, 48, 128), BF),
            pltpu.VMEM((32, 96, CHAN), BF),
            pltpu.VMEM((4, CHAN, CHAN), BF),
            pltpu.VMEM((4, CHAN, CHAN), BF),
            pltpu.VMEM((32, 96, CHAN), BF),
            pltpu.VMEM((512, 512), BF),
            pltpu.VMEM((2, 4, 4, 2, 2, 144, 128), BF),
            pltpu.VMEM((HEADS, 768, 384), F32),
            pltpu.VMEM((768, 128), F32),
            pltpu.VMEM((8, 8, 128), F32),
            pltpu.VMEM((16, 8, 128), F32),
            pltpu.VMEM((8, 768, CHAN), BF),
            pltpu.VMEM((8, 8, 128), F32),
            pltpu.VMEM((16, 8, 128), F32),
            pltpu.VMEM((16, 4, 48, CHAN), BF),
            pltpu.VMEM((4, 16, 48, CHAN), BF),
            pltpu.VMEM((3072, CHAN), BF),
            pltpu.VMEM((4, 128, 128), F32),
            pltpu.VMEM((768, CHAN), BF),
            pltpu.VMEM((6144, HEADS * 128), BF),
            pltpu.VMEM((HEADS, QROWS, 3072), BF),
            pltpu.VMEM((HEADS, WIDTH + 16, 6144), BF),
            pltpu.VMEM((CHAN, 3072), BF),
            pltpu.VMEM((CHAN, 3072), BF),
            pltpu.VMEM((2, CHAN, HEADS * 128), BF),
            pltpu.VMEM((2, 3, CHAN, CHAN), BF),
            dma((2, 3, 3)), dma((2, 3, 3)), dma((2, 4)), dma((2, 4)), dma((2, 4)), dma((2, 4)), dma((2, 4)), dma((2, 4)),
            dma((8,)), dma((8,)), dma((4,)), dma((4,)), dma((6,)), dma((6,)),
            dma(()), dma(()), dma(()), dma(()), dma((5,)), dma((6,)),
        ],
        compiler_params=pltpu.CompilerParams(collective_id=1, has_side_effects=True, vmem_limit_bytes=VLIM),
    )(*args)


def per_device(x, flags, amino, pair, pair_gain, pair_w, row_gain, row_w, row_o, col_gain, col_w, col_o):
    inc, fin = call(pair, pair_gain.reshape(1, -1), pair_w, x, flags, amino.reshape(1, -1),
                    row_gain.reshape(1, CHAN), row_w, row_o, col_gain.reshape(1, CHAN), col_w, col_o)
    upd = jnp.transpose(fin.reshape(96, 32, CHAN), (1, 0, 2))
    return inc, upd


def solution(mesh):
    ins = (P("seq", "res", None), P("seq", "res"), P("res"), P("res", "seq", None)) + (P(),) * 8
    outs = (P("seq", "res", None), P("seq", "res", None))
    return jax.shard_map(per_device, mesh=mesh, in_specs=ins, out_specs=outs, check_vma=False)
```
